32 devices in a mesh: lat: 8 (over z, x), deg: 4 (over y, core).
Axes of the slice: x: 2, y: 2, z: 4, core: 2. Of those that a mesh axis runs over, the one named last changes fastest.
Arguments:
- eta_tl: float32 [64, 10752], P('lat'), may hold values from -6 to 6
- vel_tl: float32 [2, 64, 10752], P(None, 'lat'), may hold values from -6 to 6
- eta_adj: float32 [64, 10752], P('lat'), may hold values from -6 to 6
- vel_adj: float32 [2, 64, 10752], P(None, 'lat'), may hold values from -6 to 6
- depth: float32 [64, 10752], P('lat'), may hold values from 0.2 to 1
- drag: float32 [64, 10752], P('lat'), may hold values from 0.01 to 0.3
- ocean: int32 [64, 10752], P('lat'), may hold values 0 or 1
- basis: bfloat16 [1024, 64, 1024], P('lat', None, 'deg'), may hold values from -5 to 5
- love: float32 [1024], P('deg'), may hold values from 0.05 to 0.5
Outputs:
- eta_tl_out: float32 [64, 10752], P('lat')
- vel_tl_out: float32 [2, 64, 10752], P(None, 'lat')
- eta_adj_out: float32 [64, 10752], P('lat')
- vel_adj_out: float32 [2, 64, 10752], P(None, 'lat')
The draws below stay inside these ranges and needn't reach their ends.
All inputs are finite; a program needn't handle non-finite values. No bound on the sum of `ocean` on one device may be relied on, other than what follows from the above.
Results may differ from the reference program's by a relative error of at most 0.02.
Values may be sent and summed in bfloat16 or wider, within the bound.
A program may use at most 320 MiB of HBM per device.

```python
import math
import jax
import jax.numpy as jnp
from jax import lax

NLON = 10752
MW = 1024
L = 1024
STEPS = 2
NLAT = 64


def place_ends(values, rng, smallest, high):
    dims = values.shape
    index_at = [jax.random.randint(jax.random.fold_in(rng, axis), (), 0, dims[axis]) for axis in range(len(dims))]
    values = values.at[tuple(index_at)].set(smallest)
    longest = dims.index(max(dims))
    index_at[longest] = (index_at[longest] + 1) % dims[longest]
    return values.at[tuple(index_at)].set(high)


def block_levels(own_key, shape, shards, least, high):
    def one(dim, parts):
        steps = jax.random.uniform(jax.random.fold_in(jax.random.fold_in(own_key, 6), dim), (parts,), jnp.float32, least / len(shards), high / len(shards))
        return jnp.repeat(jnp.exp(steps), shape[dim] // parts).reshape((-1,) + (1,) * (len(shape) - dim - 1))

    factor_of = one(*shards[0])
    for cut in shards[1:]:
        factor_of = factor_of * one(*cut)
    return factor_of


def noise(rng, dims, deviation, limit, split=(), kind=jnp.bfloat16):
    result = jax.random.normal(rng, dims, jnp.float32) * deviation
    if len(split) > 0:
        result = block_levels(rng, dims, split, -0.22, 0.18) * result
    return jnp.clip(result, min=-limit, max=limit).astype(kind)


def setup_inputs(seed: int = 0) -> dict:
    arg_keys = jax.random.split(jax.random.key(seed), 10)
    return {
        "eta_tl": noise(arg_keys[0], (NLAT, NLON), 1.0, 6.0, ((0, 8),), jnp.float32),
        "vel_tl": noise(arg_keys[1], (2, NLAT, NLON), 1.0, 6.0, ((1, 8),), jnp.float32),
        "eta_adj": noise(arg_keys[2], (NLAT, NLON), 1.0, 6.0, ((0, 8),), jnp.float32),
        "vel_adj": noise(arg_keys[3], (2, NLAT, NLON), 1.0, 6.0, ((1, 8),), jnp.float32),
        "depth": jnp.clip(0.2 + 0.8 * jax.random.uniform(arg_keys[4], (NLAT, NLON), jnp.float32) ** block_levels(arg_keys[4], (NLAT, NLON), ((0, 8),), -0.2, 0.2), 0.2, 1.0),
        "drag": jnp.clip(jnp.exp(math.log(0.3) - 3.4011974 * jax.random.uniform(arg_keys[5], (NLAT, NLON), jnp.float32) ** block_levels(arg_keys[5], (NLAT, NLON), ((0, 8),), -0.2, 0.2)), 0.01, 0.3),
        "ocean": place_ends((jax.random.randint(arg_keys[6], (NLAT, NLON), 0, 4) < 3).astype(jnp.int32), jax.random.fold_in(arg_keys[6], 1), 0, 1),
        "basis": noise(arg_keys[7], (MW, NLAT, L), 1.0, 5.0, ((0, 8), (2, 4))),
        "love": jnp.clip(jnp.exp(math.log(0.5) - 2.3025851 * jax.random.uniform(arg_keys[8], (L,), jnp.float32) ** block_levels(arg_keys[8], (L,), ((0, 4),), -0.2, 0.2)), 0.05, 0.5),
    }


kappa_x = 0.3
kappa_y = 0.4
block_size = 32


def load_pair(stacked, analysis_weight, output_weight, basis, love):
    rounded = lax.optimization_barrier(stacked.astype(jnp.bfloat16)).astype(jnp.float32)
    spectra = jnp.fft.rfft(rounded, axis=-1)[..., :MW] / NLON
    split_parts = jnp.stack([jnp.real(spectra), -jnp.imag(spectra)])
    split_parts = (split_parts * analysis_weight[None, :, :, None]).astype(jnp.bfloat16)
    ordered = jnp.transpose(split_parts, (3, 0, 1, 2)).reshape(MW // block_size, block_size, 2, 2, NLAT)
    basis_blocks = basis.reshape(MW // block_size, block_size, NLAT, L)

    def per_block(block_pair):
        spec_block, basis_block = block_pair
        wide_basis = basis_block.astype(jnp.float32)
        coeffs = jnp.einsum("mcfi,mil->mcfl", spec_block.astype(jnp.float32), wide_basis, precision=lax.Precision.HIGHEST)
        scaled = (coeffs * love).astype(jnp.bfloat16)
        return jnp.einsum("mcfl,mil->mcfi", scaled.astype(jnp.float32), wide_basis, precision=lax.Precision.HIGHEST).astype(jnp.bfloat16)

    synthesis = lax.map(per_block, (ordered, basis_blocks)).reshape(MW, 2, 2, NLAT).astype(jnp.float32)
    cos_part = jnp.transpose(synthesis[:, 0], (1, 2, 0))
    sin_part = jnp.transpose(synthesis[:, 1], (1, 2, 0))
    extra = NLON // 2 + 1 - MW
    padded_cos = jnp.pad(cos_part, ((0, 0), (0, 0), (0, extra)))
    padded_sin = jnp.pad(sin_part, ((0, 0), (0, 0), (0, extra)))
    grid_out = jnp.fft.irfft(padded_cos - 1j * padded_sin, n=NLON, axis=-1) * NLON
    return grid_out * output_weight[:, :, None]


def reference(eta_tl, vel_tl, eta_adj, vel_adj, depth, drag, ocean, basis, love):
    indices = jnp.arange(NLAT, dtype=jnp.int32)
    latitude = (indices.astype(jnp.float32) + 0.5) * (jnp.pi / NLAT) - 0.5 * jnp.pi
    cosine = jnp.cos(latitude)
    quad_weight = (jnp.pi / NLAT) * cosine
    east_factor = (kappa_x / (0.5 + 0.5 * cosine))[:, None]
    zero_row = jnp.zeros((1, NLON), jnp.float32)

    def north_of(values):
        return jnp.concatenate([values[1:], zero_row], 0)

    def south_of(values):
        return jnp.concatenate([zero_row, values[:-1]], 0)

    def east_of(values):
        return jnp.roll(values, -1, 1)

    def west_of(values):
        return jnp.roll(values, 1, 1)

    wet_mask = ocean.astype(jnp.float32)
    mask_u = wet_mask * east_of(wet_mask)
    mask_v = wet_mask * north_of(wet_mask)
    depth_u = 0.5 * (depth + east_of(depth))
    depth_v = 0.5 * (depth + north_of(depth))
    retain = 1.0 - drag
    ones_weight = jnp.ones_like(quad_weight)
    analysis_weight = jnp.stack([quad_weight, ones_weight])
    output_weight = jnp.stack([ones_weight, quad_weight])

    state_eta, state_vel = eta_tl, vel_tl
    back_eta, back_vel = eta_adj, vel_adj
    for step_index in range(STEPS):
        flux_east = east_factor * wet_mask * back_eta
        flux_north = kappa_y * wet_mask * back_eta
        p_term = mask_u * (back_vel[0] + depth_u * (east_of(flux_east) - flux_east))
        q_term = mask_v * (back_vel[1] + depth_v * (north_of(flux_north) - flux_north))
        flux_p = east_factor * p_term
        psi_bar = flux_p - west_of(flux_p) + kappa_y * (q_term - south_of(q_term))
        loads = load_pair(jnp.stack([state_eta, psi_bar]), analysis_weight, output_weight, basis, love)
        psi_now = state_eta - loads[0]
        new_u = mask_u * (retain * state_vel[0] - east_factor * (east_of(psi_now) - psi_now))
        new_v = mask_v * (retain * state_vel[1] - kappa_y * (north_of(psi_now) - psi_now))
        flux_x = depth_u * new_u
        flux_y = depth_v * new_v
        state_eta = state_eta - wet_mask * (east_factor * (flux_x - west_of(flux_x)) + kappa_y * (flux_y - south_of(flux_y)))
        state_vel = jnp.stack([new_u, new_v])
        back_eta = back_eta + psi_bar - loads[1]
        back_vel = jnp.stack([retain * p_term, retain * q_term])
    return state_eta, state_vel, back_eta, back_vel
```

```python
import jax
import jax.numpy as jnp
import numpy as np
from jax import lax
from jax.sharding import PartitionSpec as P

STEPS = 2
LANES = 128


kappa_x = 0.3
kappa_y = 0.4


def passed_along(value, axis, by):
    length = lax.axis_size(axis)
    pairs = [(i, i + by) for i in range(length) if 0 <= i + by < length]
    return lax.ppermute(value, axis, pairs)


def circle(numerator, period):
    angles = 2.0 * np.pi * (numerator % period) / period
    return np.cos(angles), np.sin(angles)


def fourier_tables(lon_count, order_total):
    major = lon_count // LANES
    blocks = -(-order_total // major)
    residues, lanes = np.arange(major), np.arange(LANES)
    outer = np.stack(circle(residues[:, None] * residues[None, :], major))
    turn = np.stack(circle(residues[:, None] * lanes[None, :], lon_count))
    inner = np.stack(circle(np.arange(blocks)[:, None] * lanes[None, :], LANES))
    return (
        jnp.asarray(outer, jnp.bfloat16),
        jnp.asarray(turn, jnp.float32),
        jnp.asarray(inner, jnp.bfloat16),
    )


def order_factor(orders):
    return jnp.where(orders == 0, 1.0, 2.0).astype(jnp.bfloat16)


def analyse(stacked, analysis_weight, tables, order_count):
    outer, turn, inner = tables
    row_count = stacked.shape[1]
    lon_count = stacked.shape[2]
    split_rows = stacked.astype(jnp.bfloat16).reshape(2 * row_count, lon_count // LANES, LANES)
    first = jnp.einsum("cka,rab->crkb", outer, split_rows, preferred_element_type=jnp.float32)
    turned = jnp.stack(
        [first[0] * turn[0] - first[1] * turn[1], first[1] * turn[0] + first[0] * turn[1]]
    ).astype(jnp.bfloat16)
    second = jnp.stack([jnp.stack([inner[0], -inner[1]]), jnp.stack([inner[1], inner[0]])])
    spectra = jnp.einsum("crkb,dcnb->dnkr", turned, second, preferred_element_type=jnp.float32)
    spectra = spectra.reshape(2, -1, 2, row_count)[:, :order_count] * (1.0 / lon_count)
    return (spectra * analysis_weight[None, None, :, :]).astype(jnp.bfloat16)


def legendre(spectra, basis, love):
    coeffs = jnp.einsum("cmfi,mil->cmfl", spectra, basis, preferred_element_type=jnp.float32)
    scaled = (coeffs * love[None, None, None, :]).astype(jnp.bfloat16)
    return jnp.einsum("cmfl,mil->cmfi", scaled, basis, preferred_element_type=jnp.float32)


def synthesise(coeffs, factors, tables, output_weight):
    outer, turn, inner = tables
    major, blocks = turn.shape[1], inner.shape[1]
    order_count = coeffs.shape[1]
    row_count = coeffs.shape[3]
    scaled = coeffs * factors[None, :, None, None]
    padded = jnp.pad(scaled, ((0, 0), (0, major * blocks - order_count), (0, 0), (0, 0)))
    padded = padded.reshape(2, blocks, major, 2 * row_count)
    second = jnp.stack([jnp.stack([inner[0], inner[1]]), jnp.stack([-inner[1], inner[0]])])
    first = jnp.einsum("cnkr,dcnb->drkb", padded, second, preferred_element_type=jnp.float32)
    turned = jnp.stack(
        [first[0] * turn[0] + first[1] * turn[1], first[1] * turn[0] - first[0] * turn[1]]
    ).astype(jnp.bfloat16)
    grid_out = jnp.einsum("cka,crkb->rab", outer, turned, preferred_element_type=jnp.float32)
    return grid_out.reshape(2, row_count, -1) * output_weight[:, :, None]


def edges_from(rows, by):
    sent = jnp.concatenate(rows, 0).astype(jnp.bfloat16)
    got = passed_along(sent, "lat", by).astype(jnp.float32)
    return [got[i : i + 1] for i in range(len(rows))]


def northward(values, edge):
    return jnp.concatenate([values[1:], edge], 0)


def southward(values, edge):
    return jnp.concatenate([edge, values[:-1]], 0)


def on_device(eta_tl, vel_tl, eta_adj, vel_adj, depth, drag, ocean, basis, love):
    row_count = eta_tl.shape[0]
    lon_count = eta_tl.shape[1]
    lat_count = lax.axis_size("lat")
    total_rows = row_count * lat_count
    first_row = lax.axis_index("lat") * row_count
    indices = first_row + jnp.arange(row_count, dtype=jnp.int32)
    latitude = (indices.astype(jnp.float32) + 0.5) * (jnp.pi / total_rows) - 0.5 * jnp.pi
    cosine = jnp.cos(latitude)
    quad_weight = jnp.pi / total_rows * cosine
    east_factor = (kappa_x / (0.5 + 0.5 * cosine))[:, None]
    wet_mask = ocean.astype(jnp.float32)
    flux_north = kappa_y * wet_mask * eta_adj
    north_depth, north_wet, north_flux = edges_from(
        [depth[:1], wet_mask[:1], flux_north[:1]], -1
    )
    depth_up = northward(depth, north_depth)
    wet_up = northward(wet_mask, north_wet)
    mask_u = wet_mask * jnp.roll(wet_mask, -1, 1)
    mask_v = wet_mask * wet_up
    depth_u = 0.5 * (depth + jnp.roll(depth, -1, 1))
    depth_v = 0.5 * (depth + depth_up)
    retain = 1.0 - drag
    ones_weight = jnp.ones_like(quad_weight)
    analysis_weight = jnp.stack([quad_weight, ones_weight])
    output_weight = jnp.stack([ones_weight, quad_weight])
    owned_count = basis.shape[0]
    order_total = owned_count * lat_count
    full_orders = jnp.arange(order_total, dtype=jnp.int32)
    tables = fourier_tables(lon_count, order_total)
    full_factor = order_factor(full_orders)
    state_eta, state_vel = (eta_tl, vel_tl)
    back_eta, back_vel = (eta_adj, vel_adj)

    def adjoint_terms(eta, vel, flux_edge):
        flux_east = east_factor * wet_mask * eta
        flux_up = kappa_y * wet_mask * eta
        north_up = northward(flux_up, flux_edge)
        p_term = mask_u * (vel[0] + depth_u * (jnp.roll(flux_east, -1, 1) - flux_east))
        q_term = mask_v * (vel[1] + depth_v * (north_up - flux_up))
        return p_term, q_term

    p_term, q_term = adjoint_terms(back_eta, back_vel, north_flux)
    (q_edge,) = edges_from([q_term[-1:]], 1)
    for step_index in range(STEPS):
        flux_p = east_factor * p_term
        q_down = southward(q_term, q_edge)
        psi_bar = flux_p - jnp.roll(flux_p, 1, 1) + kappa_y * (q_term - q_down)
        spectra = analyse(jnp.stack([state_eta, psi_bar]), analysis_weight, tables, order_total)
        owned_rows = lax.all_to_all(spectra, "lat", split_axis=1, concat_axis=3, tiled=True)
        partial_value = legendre(owned_rows, basis, love)
        total_sum = lax.psum(partial_value.astype(jnp.bfloat16), "deg")
        banded = lax.all_to_all(total_sum, "lat", split_axis=3, concat_axis=1, tiled=True)
        loads = synthesise(banded, full_factor, tables, output_weight)
        last = step_index == STEPS - 1
        psi_now = state_eta - loads[0]
        back_eta = back_eta + psi_bar - loads[1]
        back_vel = (retain * p_term, retain * q_term)
        north_rows = [psi_now[:1]]
        if not last:
            north_rows.append(kappa_y * wet_mask[:1] * back_eta[:1])
        north_edges = edges_from(north_rows, -1)
        psi_up = northward(psi_now, north_edges[0])
        new_u = mask_u * (
            retain * state_vel[0] - east_factor * (jnp.roll(psi_now, -1, 1) - psi_now)
        )
        new_v = mask_v * (retain * state_vel[1] - kappa_y * (psi_up - psi_now))
        flux_x = depth_u * new_u
        flux_y = depth_v * new_v
        south_rows = [flux_y[-1:]]
        if not last:
            p_term, q_term = adjoint_terms(back_eta, back_vel, north_edges[1])
            south_rows.append(q_term[-1:])
        south_edges = edges_from(south_rows, 1)
        flux_down = southward(flux_y, south_edges[0])
        if not last:
            q_edge = south_edges[1]
        state_eta = state_eta - wet_mask * (
            east_factor * (flux_x - jnp.roll(flux_x, 1, 1)) + kappa_y * (flux_y - flux_down)
        )
        state_vel = (new_u, new_v)
    state_vel, back_vel = jnp.stack(state_vel), jnp.stack(back_vel)
    return (state_eta, state_vel, back_eta, back_vel)


def solution(mesh):
    in_specs = (
        P("lat", None),
        P(None, "lat", None),
        P("lat", None),
        P(None, "lat", None),
        P("lat", None),
        P("lat", None),
        P("lat", None),
        P("lat", None, "deg"),
        P("deg"),
    )
    out_specs = (P("lat", None), P(None, "lat", None), P("lat", None), P(None, "lat", None))
    return jax.shard_map(
        on_device, mesh=mesh, in_specs=in_specs, out_specs=out_specs, check_vma=False
    )
```

```python
import functools
import jax
import jax.numpy as jnp
import numpy as np
from jax import lax
from jax.experimental import pallas as pl
from jax.experimental.pallas import tpu as pltpu
from jax.sharding import PartitionSpec as P

STEPS = 2
LANES = 128


kappa_x = 0.3
kappa_y = 0.4


def passed_along(value, axis, by):
    length = lax.axis_size(axis)
    pairs = [(i, i + by) for i in range(length) if 0 <= i + by < length]
    return lax.ppermute(value, axis, pairs)


def circle(numerator, period):
    angles = 2.0 * np.pi * (numerator % period) / period
    return np.cos(angles), np.sin(angles)


def fourier_tables(lon_count, order_total):
    major = lon_count // LANES
    blocks = -(-order_total // major)
    residues, lanes = np.arange(major), np.arange(LANES)
    outer = np.stack(circle(residues[:, None] * residues[None, :], major))
    turn = np.stack(circle(residues[:, None] * lanes[None, :], lon_count))
    inner = np.stack(circle(np.arange(blocks)[:, None] * lanes[None, :], LANES))
    return (
        jnp.asarray(outer, jnp.bfloat16),
        jnp.asarray(turn, jnp.float32),
        jnp.asarray(inner, jnp.bfloat16),
    )


def order_factor(orders):
    return jnp.where(orders == 0, 1.0, 2.0).astype(jnp.bfloat16)


def analyse(stacked, analysis_weight, tables, order_count):
    outer, turn, inner = tables
    row_count = stacked.shape[1]
    lon_count = stacked.shape[2]
    split_rows = stacked.astype(jnp.bfloat16).reshape(2 * row_count, lon_count // LANES, LANES)
    first = jnp.einsum("cka,rab->crkb", outer, split_rows, preferred_element_type=jnp.float32)
    turned = jnp.stack(
        [first[0] * turn[0] - first[1] * turn[1], first[1] * turn[0] + first[0] * turn[1]]
    ).astype(jnp.bfloat16)
    second = jnp.stack([jnp.stack([inner[0], -inner[1]]), jnp.stack([inner[1], inner[0]])])
    spectra = jnp.einsum("crkb,dcnb->drnk", turned, second, preferred_element_type=jnp.float32)
    spectra = spectra.reshape(2, 2, row_count, -1)[..., :order_count] * (1.0 / lon_count)
    return (spectra * analysis_weight[None, :, :, None]).astype(jnp.bfloat16)


def legendre(spectra, basis, love):
    coeffs = jnp.einsum("cmfi,mil->cmfl", spectra, basis, preferred_element_type=jnp.float32)
    scaled = (coeffs * love[None, None, None, :]).astype(jnp.bfloat16)
    return jnp.einsum("cmfl,mil->cmfi", scaled, basis, preferred_element_type=jnp.float32)


def synthesise(coeffs, factors, tables, output_weight):
    outer, turn, inner = tables
    major, blocks = turn.shape[1], inner.shape[1]
    row_count, order_count = coeffs.shape[2:]
    scaled = (coeffs * factors).reshape(2, 2 * row_count, order_count)
    padded = jnp.pad(scaled, ((0, 0), (0, 0), (0, major * blocks - order_count)))
    padded = padded.reshape(2, 2 * row_count, blocks, major)
    second = jnp.stack([jnp.stack([inner[0], inner[1]]), jnp.stack([-inner[1], inner[0]])])
    first = jnp.einsum("crnk,dcnb->drkb", padded, second, preferred_element_type=jnp.float32)
    turned = jnp.stack(
        [first[0] * turn[0] + first[1] * turn[1], first[1] * turn[0] - first[0] * turn[1]]
    ).astype(jnp.bfloat16)
    grid_out = jnp.einsum("cka,crkb->rab", outer, turned, preferred_element_type=jnp.float32)
    return grid_out.reshape(2, row_count, -1) * output_weight[:, :, None]


def greet(count, device_of):
    barrier = pltpu.get_barrier_semaphore()

    def one(step, carry):
        pl.semaphore_signal(
            barrier, inc=1, device_id=device_of(step), device_id_type=pl.DeviceIdType.MESH
        )
        return carry

    lax.fori_loop(1, count, one, 0)
    pl.semaphore_wait(barrier, count - 1)


def swap(count, copy_of):
    def begin(step, carry):
        copy_of(step).start()
        return carry

    def finish(step, carry):
        copy_of(step).wait()
        return carry

    lax.fori_loop(1, count, begin, 0)
    return lambda: lax.fori_loop(1, count, finish, 0)


def spread_kernel(lat_count, send_ref, out_ref, held, send_sem, recv_sem):
    me_lat, me_deg = lax.axis_index("lat"), lax.axis_index("deg")

    def device_of(step):
        return (lax.rem(me_lat + step, lat_count), me_deg)

    def copy_of(step):
        peer = device_of(step)
        return pltpu.make_async_remote_copy(
            src_ref=send_ref.at[peer[0]],
            dst_ref=held.at[me_lat],
            send_sem=send_sem.at[step - 1],
            recv_sem=recv_sem.at[step - 1],
            device_id=peer,
            device_id_type=pl.DeviceIdType.MESH,
        )

    greet(lat_count, device_of)
    finish = swap(lat_count, copy_of)
    held[me_lat] = send_ref[me_lat]
    finish()
    out_ref[...] = held[...]


def gather_kernel(lat_count, deg_count, send_ref, out_ref, held, send_sem, recv_sem):
    count = lat_count * deg_count
    me_lat, me_deg = lax.axis_index("lat"), lax.axis_index("deg")
    me = me_lat * deg_count + me_deg

    def device_of(step):
        peer = lax.rem(me + step, count)
        return (lax.div(peer, deg_count), lax.rem(peer, deg_count))

    def copy_of(step):
        peer = device_of(step)
        return pltpu.make_async_remote_copy(
            src_ref=send_ref.at[peer[0]],
            dst_ref=held.at[me],
            send_sem=send_sem.at[step - 1],
            recv_sem=recv_sem.at[step - 1],
            device_id=peer,
            device_id_type=pl.DeviceIdType.MESH,
        )

    greet(count, device_of)
    finish = swap(count, copy_of)
    held[me] = send_ref[me_lat]
    finish()
    for source in range(lat_count):
        total = held[source * deg_count].astype(jnp.float32)
        for part in range(1, deg_count):
            total = total + held[source * deg_count + part].astype(jnp.float32)
        out_ref[source] = total.astype(out_ref.dtype)


def exchange(kernel, count, peers, blocks, collective_id):
    return pl.pallas_call(
        kernel,
        out_shape=jax.ShapeDtypeStruct(blocks.shape, blocks.dtype),
        in_specs=[pl.BlockSpec(memory_space=pltpu.VMEM)],
        out_specs=pl.BlockSpec(memory_space=pltpu.VMEM),
        scratch_shapes=[
            pltpu.VMEM((count,) + blocks.shape[1:], blocks.dtype),
            pltpu.SemaphoreType.DMA((peers - 1,)),
            pltpu.SemaphoreType.DMA((peers - 1,)),
        ],
        compiler_params=pltpu.CompilerParams(collective_id=collective_id, has_side_effects=True),
    )(blocks)


def spread_orders(spectra, lat_count):
    row_count, order_total = spectra.shape[2:]
    owned = order_total // lat_count
    blocks = spectra.reshape(4 * row_count, lat_count, owned).transpose(1, 0, 2)
    kernel = functools.partial(spread_kernel, lat_count)
    got = exchange(kernel, lat_count, lat_count, blocks, 0)
    got = got.reshape(lat_count, 2, 2, row_count, owned).transpose(1, 4, 2, 0, 3)
    return got.reshape(2, owned, 2, lat_count * row_count)


def gather_rows(partial_value, lat_count, deg_count):
    owned, total_rows = partial_value.shape[1], partial_value.shape[3]
    row_count = total_rows // lat_count
    blocks = partial_value.reshape(2, owned, 2, lat_count, row_count).transpose(3, 0, 2, 4, 1)
    blocks = blocks.reshape(lat_count, 4 * row_count, owned)
    kernel = functools.partial(gather_kernel, lat_count, deg_count)
    count = lat_count * deg_count
    got = exchange(kernel, count, count, blocks, 1)
    return got.transpose(1, 0, 2).reshape(2, 2, row_count, lat_count * owned)


def edges_from(rows, by):
    sent = jnp.concatenate(rows, 0).astype(jnp.bfloat16)
    got = passed_along(sent, "lat", by).astype(jnp.float32)
    return [got[i : i + 1] for i in range(len(rows))]


def northward(values, edge):
    return jnp.concatenate([values[1:], edge], 0)


def southward(values, edge):
    return jnp.concatenate([edge, values[:-1]], 0)


def on_device(eta_tl, vel_tl, eta_adj, vel_adj, depth, drag, ocean, basis, love):
    row_count = eta_tl.shape[0]
    lon_count = eta_tl.shape[1]
    lat_count = lax.axis_size("lat")
    total_rows = row_count * lat_count
    first_row = lax.axis_index("lat") * row_count
    indices = first_row + jnp.arange(row_count, dtype=jnp.int32)
    latitude = (indices.astype(jnp.float32) + 0.5) * (jnp.pi / total_rows) - 0.5 * jnp.pi
    cosine = jnp.cos(latitude)
    quad_weight = jnp.pi / total_rows * cosine
    east_factor = (kappa_x / (0.5 + 0.5 * cosine))[:, None]
    wet_mask = ocean.astype(jnp.float32)
    flux_north = kappa_y * wet_mask * eta_adj
    north_depth, north_wet, north_flux = edges_from(
        [depth[:1], wet_mask[:1], flux_north[:1]], -1
    )
    depth_up = northward(depth, north_depth)
    wet_up = northward(wet_mask, north_wet)
    mask_u = wet_mask * jnp.roll(wet_mask, -1, 1)
    mask_v = wet_mask * wet_up
    depth_u = 0.5 * (depth + jnp.roll(depth, -1, 1))
    depth_v = 0.5 * (depth + depth_up)
    retain = 1.0 - drag
    ones_weight = jnp.ones_like(quad_weight)
    analysis_weight = jnp.stack([quad_weight, ones_weight])
    output_weight = jnp.stack([ones_weight, quad_weight])
    owned_count = basis.shape[0]
    order_total = owned_count * lat_count
    full_orders = jnp.arange(order_total, dtype=jnp.int32)
    tables = fourier_tables(lon_count, order_total)
    full_factor = order_factor(full_orders)
    state_eta, state_vel = (eta_tl, vel_tl)
    back_eta, back_vel = (eta_adj, vel_adj)

    def adjoint_terms(eta, vel, flux_edge):
        flux_east = east_factor * wet_mask * eta
        flux_up = kappa_y * wet_mask * eta
        north_up = northward(flux_up, flux_edge)
        p_term = mask_u * (vel[0] + depth_u * (jnp.roll(flux_east, -1, 1) - flux_east))
        q_term = mask_v * (vel[1] + depth_v * (north_up - flux_up))
        return p_term, q_term

    p_term, q_term = adjoint_terms(back_eta, back_vel, north_flux)
    (q_edge,) = edges_from([q_term[-1:]], 1)
    for step_index in range(STEPS):
        flux_p = east_factor * p_term
        q_down = southward(q_term, q_edge)
        psi_bar = flux_p - jnp.roll(flux_p, 1, 1) + kappa_y * (q_term - q_down)
        spectra = analyse(jnp.stack([state_eta, psi_bar]), analysis_weight, tables, order_total)
        owned_rows = spread_orders(spectra, lat_count)
        partial_value = legendre(owned_rows, basis, love).astype(jnp.bfloat16)
        banded = gather_rows(partial_value, lat_count, lax.axis_size("deg"))
        loads = synthesise(banded, full_factor, tables, output_weight)
        last = step_index == STEPS - 1
        psi_now = state_eta - loads[0]
        back_eta = back_eta + psi_bar - loads[1]
        back_vel = (retain * p_term, retain * q_term)
        north_rows = [psi_now[:1]]
        if not last:
            north_rows.append(kappa_y * wet_mask[:1] * back_eta[:1])
        north_edges = edges_from(north_rows, -1)
        psi_up = northward(psi_now, north_edges[0])
        new_u = mask_u * (
            retain * state_vel[0] - east_factor * (jnp.roll(psi_now, -1, 1) - psi_now)
        )
        new_v = mask_v * (retain * state_vel[1] - kappa_y * (psi_up - psi_now))
        flux_x = depth_u * new_u
        flux_y = depth_v * new_v
        south_rows = [flux_y[-1:]]
        if not last:
            p_term, q_term = adjoint_terms(back_eta, back_vel, north_edges[1])
            south_rows.append(q_term[-1:])
        south_edges = edges_from(south_rows, 1)
        flux_down = southward(flux_y, south_edges[0])
        if not last:
            q_edge = south_edges[1]
        state_eta = state_eta - wet_mask * (
            east_factor * (flux_x - jnp.roll(flux_x, 1, 1)) + kappa_y * (flux_y - flux_down)
        )
        state_vel = (new_u, new_v)
    state_vel, back_vel = jnp.stack(state_vel), jnp.stack(back_vel)
    return (state_eta, state_vel, back_eta, back_vel)


def solution(mesh):
    in_specs = (
        P("lat", None),
        P(None, "lat", None),
        P("lat", None),
        P(None, "lat", None),
        P("lat", None),
        P("lat", None),
        P("lat", None),
        P("lat", None, "deg"),
        P("deg"),
    )
    out_specs = (P("lat", None), P(None, "lat", None), P("lat", None), P(None, "lat", None))
    return jax.shard_map(
        on_device, mesh=mesh, in_specs=in_specs, out_specs=out_specs, check_vma=False
    )
```

```python
import functools
import jax
import jax.numpy as jnp
import numpy as np
from jax import lax
from jax.experimental import pallas as pl
from jax.experimental.pallas import tpu as pltpu
from jax.sharding import PartitionSpec as P

STEPS = 2
LANES = 128


kappa_x = 0.3
kappa_y = 0.4


def passed_along(value, axis, by):
    length = lax.axis_size(axis)
    pairs = [(i, i + by) for i in range(length) if 0 <= i + by < length]
    return lax.ppermute(value, axis, pairs)


def circle(numerator, period):
    angles = 2.0 * np.pi * (numerator % period) / period
    return np.cos(angles), np.sin(angles)


def fourier_tables(lon_count, order_total):
    major = lon_count // LANES
    blocks = -(-order_total // major)
    residues, lanes = np.arange(major), np.arange(LANES)
    outer = np.stack(circle(residues[:, None] * residues[None, :], major))
    turn = np.stack(circle(residues[:, None] * lanes[None, :], lon_count))
    inner = np.stack(circle(np.arange(blocks)[:, None] * lanes[None, :], LANES))
    return (
        jnp.asarray(outer, jnp.bfloat16),
        jnp.asarray(turn, jnp.float32),
        jnp.asarray(inner, jnp.bfloat16),
    )


def order_factor(orders):
    return jnp.where(orders == 0, 1.0, 2.0).astype(jnp.bfloat16)


def analyse(stacked, analysis_weight, tables, order_count):
    outer, turn, inner = tables
    row_count = stacked.shape[1]
    lon_count = stacked.shape[2]
    split_rows = stacked.astype(jnp.bfloat16).reshape(2 * row_count, lon_count // LANES, LANES)
    first = jnp.einsum("cka,rab->crkb", outer, split_rows, preferred_element_type=jnp.float32)
    turned = jnp.stack(
        [first[0] * turn[0] - first[1] * turn[1], first[1] * turn[0] + first[0] * turn[1]]
    ).astype(jnp.bfloat16)
    second = jnp.stack([jnp.stack([inner[0], -inner[1]]), jnp.stack([inner[1], inner[0]])])
    spectra = jnp.einsum("crkb,dcnb->drnk", turned, second, preferred_element_type=jnp.float32)
    spectra = spectra.reshape(2, 2, row_count, -1)[..., :order_count] * (1.0 / lon_count)
    return (spectra * analysis_weight[None, :, :, None]).astype(jnp.bfloat16)


def legendre(spectra, basis, love):
    coeffs = jnp.einsum("cmfi,mil->cmfl", spectra, basis, preferred_element_type=jnp.float32)
    scaled = (coeffs * love[None, None, None, :]).astype(jnp.bfloat16)
    return jnp.einsum("cmfl,mil->cmfi", scaled, basis, preferred_element_type=jnp.float32)


def synthesise(coeffs, factors, tables, output_weight):
    outer, turn, inner = tables
    major, blocks = turn.shape[1], inner.shape[1]
    row_count, order_count = coeffs.shape[2:]
    scaled = (coeffs * factors).reshape(2, 2 * row_count, order_count)
    padded = jnp.pad(scaled, ((0, 0), (0, 0), (0, major * blocks - order_count)))
    padded = padded.reshape(2, 2 * row_count, blocks, major)
    second = jnp.stack([jnp.stack([inner[0], inner[1]]), jnp.stack([-inner[1], inner[0]])])
    first = jnp.einsum("crnk,dcnb->drkb", padded, second, preferred_element_type=jnp.float32)
    turned = jnp.stack(
        [first[0] * turn[0] + first[1] * turn[1], first[1] * turn[0] - first[0] * turn[1]]
    ).astype(jnp.bfloat16)
    grid_out = jnp.einsum("cka,crkb->rab", outer, turned, preferred_element_type=jnp.float32)
    return grid_out.reshape(2, row_count, -1) * output_weight[:, :, None]


def greet(count, device_of):
    barrier = pltpu.get_barrier_semaphore()

    def one(step, carry):
        pl.semaphore_signal(
            barrier, inc=1, device_id=device_of(step), device_id_type=pl.DeviceIdType.MESH
        )
        return carry

    lax.fori_loop(1, count, one, 0)
    pl.semaphore_wait(barrier, count - 1)


def swap(count, copy_of):
    def begin(step, carry):
        copy_of(step).start()
        return carry

    def finish(step, carry):
        copy_of(step).wait()
        return carry

    lax.fori_loop(1, count, begin, 0)
    return lambda: lax.fori_loop(1, count, finish, 0)


def spread_kernel(lat_count, send_ref, out_ref, held, send_sem, recv_sem):
    me_lat, me_deg = lax.axis_index("lat"), lax.axis_index("deg")

    def device_of(step):
        return (lax.rem(me_lat + step, lat_count), me_deg)

    def copy_of(step):
        peer = device_of(step)
        return pltpu.make_async_remote_copy(
            src_ref=send_ref.at[peer[0]],
            dst_ref=held.at[me_lat],
            send_sem=send_sem.at[step - 1],
            recv_sem=recv_sem.at[step - 1],
            device_id=peer,
            device_id_type=pl.DeviceIdType.MESH,
        )

    greet(lat_count, device_of)
    finish = swap(lat_count, copy_of)
    held[me_lat] = send_ref[me_lat]
    finish()
    out_ref[...] = held[...]


def gather_kernel(lat_count, deg_count, send_ref, out_ref, held, send_sem, recv_sem):
    count = lat_count * deg_count
    me_lat, me_deg = lax.axis_index("lat"), lax.axis_index("deg")
    me = me_lat * deg_count + me_deg

    def device_of(step):
        peer = lax.rem(me + step, count)
        return (lax.div(peer, deg_count), lax.rem(peer, deg_count))

    def copy_of(step):
        peer = device_of(step)
        return pltpu.make_async_remote_copy(
            src_ref=send_ref.at[peer[0]],
            dst_ref=held.at[me],
            send_sem=send_sem.at[step - 1],
            recv_sem=recv_sem.at[step - 1],
            device_id=peer,
            device_id_type=pl.DeviceIdType.MESH,
        )

    greet(count, device_of)
    finish = swap(count, copy_of)
    held[me] = send_ref[me_lat]
    finish()
    for source in range(lat_count):
        total = held[source * deg_count].astype(jnp.float32)
        for part in range(1, deg_count):
            total = total + held[source * deg_count + part].astype(jnp.float32)
        out_ref[source] = total.astype(out_ref.dtype)


def exchange(kernel, count, peers, blocks, collective_id):
    return pl.pallas_call(
        kernel,
        out_shape=jax.ShapeDtypeStruct(blocks.shape, blocks.dtype),
        in_specs=[pl.BlockSpec(memory_space=pltpu.VMEM)],
        out_specs=pl.BlockSpec(memory_space=pltpu.VMEM),
        scratch_shapes=[
            pltpu.VMEM((count,) + blocks.shape[1:], blocks.dtype),
            pltpu.SemaphoreType.DMA((peers - 1,)),
            pltpu.SemaphoreType.DMA((peers - 1,)),
        ],
        compiler_params=pltpu.CompilerParams(collective_id=collective_id, has_side_effects=True),
    )(blocks)


def spread_orders(spectra, lat_count):
    row_count, order_total = spectra.shape[2:]
    owned = order_total // lat_count
    blocks = spectra.reshape(4 * row_count, lat_count, owned).transpose(1, 0, 2)
    kernel = functools.partial(spread_kernel, lat_count)
    got = exchange(kernel, lat_count, lat_count, blocks, 0)
    got = got.reshape(lat_count, 2, 2, row_count, owned).transpose(1, 4, 2, 0, 3)
    return got.reshape(2, owned, 2, lat_count * row_count)


def gather_rows(partial_value, lat_count, deg_count):
    owned, total_rows = partial_value.shape[1], partial_value.shape[3]
    row_count = total_rows // lat_count
    blocks = partial_value.reshape(2, owned, 2, lat_count, row_count).transpose(3, 0, 2, 4, 1)
    blocks = blocks.reshape(lat_count, 4 * row_count, owned)
    kernel = functools.partial(gather_kernel, lat_count, deg_count)
    count = lat_count * deg_count
    got = exchange(kernel, count, count, blocks, 1)
    return got.transpose(1, 0, 2).reshape(2, 2, row_count, lat_count * owned)


def edges_from(rows, by):
    sent = jnp.concatenate(rows, 0).astype(jnp.bfloat16)
    got = passed_along(sent, "lat", by).astype(jnp.float32)
    return [got[i : i + 1] for i in range(len(rows))]


def northward(values, edge):
    return jnp.concatenate([values[1:], edge], 0)


def southward(values, edge):
    return jnp.concatenate([edge, values[:-1]], 0)


def on_device(eta_tl, vel_tl, eta_adj, vel_adj, depth, drag, ocean, basis, love):
    row_count = eta_tl.shape[0]
    lon_count = eta_tl.shape[1]
    lat_count = lax.axis_size("lat")
    total_rows = row_count * lat_count
    first_row = lax.axis_index("lat") * row_count
    indices = first_row + jnp.arange(row_count, dtype=jnp.int32)
    latitude = (indices.astype(jnp.float32) + 0.5) * (jnp.pi / total_rows) - 0.5 * jnp.pi
    cosine = jnp.cos(latitude)
    quad_weight = jnp.pi / total_rows * cosine
    east_factor = (kappa_x / (0.5 + 0.5 * cosine))[:, None]
    wet_mask = ocean.astype(jnp.float32)
    flux_north = kappa_y * wet_mask * eta_adj
    north_depth, north_wet, north_flux = edges_from(
        [depth[:1], wet_mask[:1], flux_north[:1]], -1
    )
    south_flux, south_depth, south_wet, south_drag, south_v, south_va = edges_from(
        [flux_north[-1:], depth[-1:], wet_mask[-1:], drag[-1:], vel_tl[1, -1:], vel_adj[1, -1:]], 1
    )
    south_mask = south_wet * wet_mask[:1]
    south_height = 0.5 * (south_depth + depth[:1])
    south_retain = 1.0 - south_drag
    depth_up = northward(depth, north_depth)
    wet_up = northward(wet_mask, north_wet)
    mask_u = wet_mask * jnp.roll(wet_mask, -1, 1)
    mask_v = wet_mask * wet_up
    depth_u = 0.5 * (depth + jnp.roll(depth, -1, 1))
    depth_v = 0.5 * (depth + depth_up)
    retain = 1.0 - drag
    ones_weight = jnp.ones_like(quad_weight)
    analysis_weight = jnp.stack([quad_weight, ones_weight])
    output_weight = jnp.stack([ones_weight, quad_weight])
    owned_count = basis.shape[0]
    order_total = owned_count * lat_count
    full_orders = jnp.arange(order_total, dtype=jnp.int32)
    tables = fourier_tables(lon_count, order_total)
    full_factor = order_factor(full_orders)
    state_eta, state_vel = (eta_tl, vel_tl)
    back_eta, back_vel = (eta_adj, vel_adj)

    def adjoint_terms(eta, vel, flux_edge, flux_below, va_below):
        flux_east = east_factor * wet_mask * eta
        flux_up = kappa_y * wet_mask * eta
        north_up = northward(flux_up, flux_edge)
        p_term = mask_u * (vel[0] + depth_u * (jnp.roll(flux_east, -1, 1) - flux_east))
        q_term = mask_v * (vel[1] + depth_v * (north_up - flux_up))
        q_below = south_mask * (va_below + south_height * (flux_up[:1] - flux_below))
        return p_term, q_term, q_below

    p_term, q_term, q_edge = adjoint_terms(back_eta, back_vel, north_flux, south_flux, south_va)
    for step_index in range(STEPS):
        flux_p = east_factor * p_term
        q_down = southward(q_term, q_edge)
        psi_bar = flux_p - jnp.roll(flux_p, 1, 1) + kappa_y * (q_term - q_down)
        spectra = analyse(jnp.stack([state_eta, psi_bar]), analysis_weight, tables, order_total)
        owned_rows = spread_orders(spectra, lat_count)
        partial_value = legendre(owned_rows, basis, love).astype(jnp.bfloat16)
        banded = gather_rows(partial_value, lat_count, lax.axis_size("deg"))
        loads = synthesise(banded, full_factor, tables, output_weight)
        last = step_index == STEPS - 1
        psi_now = state_eta - loads[0]
        back_eta = back_eta + psi_bar - loads[1]
        back_vel = (retain * p_term, retain * q_term)
        north_rows, south_rows = [psi_now[:1]], [psi_now[-1:]]
        if not last:
            flux_now = kappa_y * wet_mask * back_eta
            north_rows.append(flux_now[:1])
            south_rows.append(flux_now[-1:])
        north_edges = edges_from(north_rows, -1)
        south_edges = edges_from(south_rows, 1)
        psi_up = northward(psi_now, north_edges[0])
        new_u = mask_u * (
            retain * state_vel[0] - east_factor * (jnp.roll(psi_now, -1, 1) - psi_now)
        )
        new_v = mask_v * (retain * state_vel[1] - kappa_y * (psi_up - psi_now))
        flux_x = depth_u * new_u
        flux_y = depth_v * new_v
        south_v = south_mask * (south_retain * south_v - kappa_y * (psi_now[:1] - south_edges[0]))
        flux_down = southward(flux_y, south_height * south_v)
        if not last:
            south_va = south_retain * q_edge
            p_term, q_term, q_edge = adjoint_terms(
                back_eta, back_vel, north_edges[1], south_edges[1], south_va
            )
        state_eta = state_eta - wet_mask * (
            east_factor * (flux_x - jnp.roll(flux_x, 1, 1)) + kappa_y * (flux_y - flux_down)
        )
        state_vel = (new_u, new_v)
    state_vel, back_vel = jnp.stack(state_vel), jnp.stack(back_vel)
    return (state_eta, state_vel, back_eta, back_vel)


def solution(mesh):
    in_specs = (
        P("lat", None),
        P(None, "lat", None),
        P("lat", None),
        P(None, "lat", None),
        P("lat", None),
        P("lat", None),
        P("lat", None),
        P("lat", None, "deg"),
        P("deg"),
    )
    out_specs = (P("lat", None), P(None, "lat", None), P("lat", None), P(None, "lat", None))
    return jax.shard_map(
        on_device, mesh=mesh, in_specs=in_specs, out_specs=out_specs, check_vma=False
    )
```

```python
import functools
import jax
import jax.numpy as jnp
import numpy as np
from jax import lax
from jax.experimental import pallas as pl
from jax.experimental.pallas import tpu as pltpu
from jax.sharding import PartitionSpec as P

STEPS = 2
LANES = 128
GROUP = 32


kappa_x = 0.3
kappa_y = 0.4


def passed_along(value, axis, by):
    length = lax.axis_size(axis)
    pairs = [(i, i + by) for i in range(length) if 0 <= i + by < length]
    return lax.ppermute(value, axis, pairs)


def circle(numerator, period):
    angles = 2.0 * np.pi * (numerator % period) / period
    return np.cos(angles), np.sin(angles)


def fourier_tables(lon_count, order_total):
    major = lon_count // LANES
    blocks = -(-order_total // major)
    residues, lanes = np.arange(major), np.arange(LANES)
    outer = np.stack(circle(residues[:, None] * residues[None, :], major))
    turn = np.stack(circle(residues[:, None] * lanes[None, :], lon_count))
    inner = np.stack(circle(np.arange(blocks)[:, None] * lanes[None, :], LANES))
    return (
        jnp.asarray(outer, jnp.bfloat16),
        jnp.asarray(turn, jnp.float32),
        jnp.asarray(inner, jnp.bfloat16),
    )


def order_factor(orders):
    return jnp.where(orders == 0, 1.0, 2.0).astype(jnp.bfloat16)


def analyse(stacked, analysis_weight, tables, order_count):
    outer, turn, inner = tables
    row_count = stacked.shape[1]
    lon_count = stacked.shape[2]
    split_rows = stacked.astype(jnp.bfloat16).reshape(2 * row_count, lon_count // LANES, LANES)
    first = jnp.einsum("cka,rab->crkb", outer, split_rows, preferred_element_type=jnp.float32)
    turned = jnp.stack(
        [first[0] * turn[0] - first[1] * turn[1], first[1] * turn[0] + first[0] * turn[1]]
    ).astype(jnp.bfloat16)
    second = jnp.stack([jnp.stack([inner[0], -inner[1]]), jnp.stack([inner[1], inner[0]])])
    spectra = jnp.einsum("crkb,dcnb->drnk", turned, second, preferred_element_type=jnp.float32)
    spectra = spectra.reshape(2, 2, row_count, -1)[..., :order_count] * (1.0 / lon_count)
    return (spectra * analysis_weight[None, :, :, None]).astype(jnp.bfloat16)


def synthesise(coeffs, factors, tables, output_weight):
    outer, turn, inner = tables
    major, blocks = turn.shape[1], inner.shape[1]
    row_count, order_count = coeffs.shape[2:]
    scaled = (coeffs * factors).reshape(2, 2 * row_count, order_count)
    padded = jnp.pad(scaled, ((0, 0), (0, 0), (0, major * blocks - order_count)))
    padded = padded.reshape(2, 2 * row_count, blocks, major)
    second = jnp.stack([jnp.stack([inner[0], inner[1]]), jnp.stack([-inner[1], inner[0]])])
    first = jnp.einsum("crnk,dcnb->drkb", padded, second, preferred_element_type=jnp.float32)
    turned = jnp.stack(
        [first[0] * turn[0] + first[1] * turn[1], first[1] * turn[0] - first[0] * turn[1]]
    ).astype(jnp.bfloat16)
    grid_out = jnp.einsum("cka,crkb->rab", outer, turned, preferred_element_type=jnp.float32)
    return grid_out.reshape(2, row_count, -1) * output_weight[:, :, None]


def greet(count, device_of):
    barrier = pltpu.get_barrier_semaphore()

    def one(step, carry):
        pl.semaphore_signal(
            barrier, inc=1, device_id=device_of(step), device_id_type=pl.DeviceIdType.MESH
        )
        return carry

    lax.fori_loop(1, count, one, 0)
    pl.semaphore_wait(barrier, count - 1)


def swap(count, copy_of):
    def begin(step, carry):
        copy_of(step).start()
        return carry

    def finish(step, carry):
        copy_of(step).wait()
        return carry

    lax.fori_loop(1, count, begin, 0)
    return lambda: lax.fori_loop(1, count, finish, 0)


def load_kernel(
    sizes, send_ref, basis_ref, love_ref, out_ref, basis, landed, ready, held,
    basis_sem, spread_out, spread_in, gather_out, gather_in,
):
    lat_count, deg_count, row_count, halves, cluster = sizes
    tall = 4 * cluster
    count = lat_count * deg_count
    total_rows = lat_count * row_count
    me_lat, me_deg = lax.axis_index("lat"), lax.axis_index("deg")
    me = me_lat * deg_count + me_deg

    def band_of(step):
        return (lax.rem(me_lat + step, lat_count), me_deg)

    def device_of(step):
        peer = lax.rem(me + step, count)
        return (lax.div(peer, deg_count), lax.rem(peer, deg_count))

    def spread_copy(step):
        peer = band_of(step)
        return pltpu.make_async_remote_copy(
            src_ref=send_ref.at[peer[0]],
            dst_ref=landed.at[me_lat],
            send_sem=spread_out.at[step - 1],
            recv_sem=spread_in.at[step - 1],
            device_id=peer,
            device_id_type=pl.DeviceIdType.MESH,
        )

    def gather_copy(step):
        peer = device_of(step)
        return pltpu.make_async_remote_copy(
            src_ref=ready.at[peer[0]],
            dst_ref=held.at[me],
            send_sem=gather_out.at[step - 1],
            recv_sem=gather_in.at[step - 1],
            device_id=peer,
            device_id_type=pl.DeviceIdType.MESH,
        )

    fetch = pltpu.make_async_copy(basis_ref, basis, basis_sem)
    fetch.start()
    greet(count, device_of)
    finish = swap(lat_count, spread_copy)
    landed[me_lat] = send_ref[me_lat]
    finish()
    fetch.wait()

    copies = max(1, LANES // total_rows)
    width = copies * total_rows
    row_order = lax.broadcasted_iota(jnp.int32, (tall, width), 0) % cluster
    lane_part = lax.broadcasted_iota(jnp.int32, (tall, width), 1) // total_rows
    chunk = min(cluster, max(copies, 2048 // total_rows))
    blocks = [landed[source].astype(jnp.float32) for source in range(lat_count)]
    groups = blocks[0].shape[1] // tall
    love = love_ref[...]
    done = []
    for half in range(halves):
        for group in range(groups):
            first = (half * groups + group) * cluster
            lanes = slice(group * tall, (group + 1) * tall)
            rows = slice(half * row_count, (half + 1) * row_count)
            tile = jnp.concatenate([block[rows, lanes] for block in blocks], 0).T
            tile = jnp.concatenate([tile] * copies, 1)
            masks = [row_order == order + lane_part for order in range(0, cluster, copies)]
            total = jnp.zeros((tall, love.shape[1]), jnp.float32)
            for start in range(0, cluster, chunk):
                spaced = jnp.concatenate(
                    [
                        jnp.where(masks[order // copies], tile, 0.0).astype(jnp.bfloat16)
                        for order in range(start, start + chunk, copies)
                    ],
                    1,
                )
                part = basis[first + start : first + start + chunk]
                part = part.reshape(chunk * total_rows, love.shape[1])
                total = total + jnp.dot(spaced, part, preferred_element_type=jnp.float32)
            scaled = (total * love).astype(jnp.bfloat16)
            merged = jnp.zeros((tall, width), jnp.float32)
            for start in range(0, cluster, chunk):
                part = basis[first + start : first + start + chunk]
                part = part.reshape(chunk * total_rows, love.shape[1])
                wide = lax.dot_general(
                    scaled, part, (((1,), (1,)), ((), ())), preferred_element_type=jnp.float32
                )
                for step in range(chunk // copies):
                    mask = masks[start // copies + step]
                    merged = merged + jnp.where(
                        mask, wide[:, step * width : (step + 1) * width], 0.0
                    )
            summed = merged[:, :total_rows]
            for copy in range(1, copies):
                summed = summed + merged[:, copy * total_rows : (copy + 1) * total_rows]
            done.append(summed.T)
    for band in range(lat_count):
        rows = slice(band * row_count, (band + 1) * row_count)
        lines = [
            jnp.concatenate([done[half * groups + g][rows] for g in range(groups)], 1)
            for half in range(halves)
        ]
        ready[band] = jnp.concatenate(lines, 0).astype(jnp.bfloat16)
    finish = swap(count, gather_copy)
    held[me] = ready[me_lat]
    finish()
    for source in range(lat_count):
        total = held[source * deg_count].astype(jnp.float32)
        for part in range(1, deg_count):
            total = total + held[source * deg_count + part].astype(jnp.float32)
        out_ref[source] = total.astype(out_ref.dtype)


def load_spectra(spectra, basis, love, lat_count, deg_count):
    row_count, order_total = spectra.shape[2:]
    owned = order_total // lat_count
    halves = max(1, 16 // row_count)
    cluster = min(GROUP, owned // halves)
    groups = owned // (halves * cluster)
    split = spectra.reshape(2, 2, row_count, lat_count, halves, groups, cluster)
    blocks = split.transpose(3, 4, 2, 5, 0, 1, 6)
    blocks = blocks.reshape(lat_count, halves * row_count, groups * 4 * cluster)
    count = lat_count * deg_count
    vmem = pl.BlockSpec(memory_space=pltpu.VMEM)
    got = pl.pallas_call(
        functools.partial(load_kernel, (lat_count, deg_count, row_count, halves, cluster)),
        out_shape=jax.ShapeDtypeStruct(blocks.shape, blocks.dtype),
        in_specs=[vmem, pl.BlockSpec(memory_space=pl.ANY), vmem],
        out_specs=vmem,
        scratch_shapes=[
            pltpu.VMEM(basis.shape, basis.dtype),
            pltpu.VMEM(blocks.shape, blocks.dtype),
            pltpu.VMEM(blocks.shape, blocks.dtype),
            pltpu.VMEM((count,) + blocks.shape[1:], blocks.dtype),
            pltpu.SemaphoreType.DMA,
            pltpu.SemaphoreType.DMA((lat_count - 1,)),
            pltpu.SemaphoreType.DMA((lat_count - 1,)),
            pltpu.SemaphoreType.DMA((count - 1,)),
            pltpu.SemaphoreType.DMA((count - 1,)),
        ],
        compiler_params=pltpu.CompilerParams(
            collective_id=0, has_side_effects=True, vmem_limit_bytes=40 * 2**20
        ),
    )(blocks, basis, love[None, :])
    got = got.reshape(lat_count, halves, row_count, groups, 2, 2, cluster)
    return got.transpose(4, 5, 2, 0, 1, 3, 6).reshape(spectra.shape)


def edges_from(rows, by):
    sent = jnp.concatenate(rows, 0).astype(jnp.bfloat16)
    got = passed_along(sent, "lat", by).astype(jnp.float32)
    return [got[i : i + 1] for i in range(len(rows))]


def northward(values, edge):
    return jnp.concatenate([values[1:], edge], 0)


def southward(values, edge):
    return jnp.concatenate([edge, values[:-1]], 0)


def on_device(eta_tl, vel_tl, eta_adj, vel_adj, depth, drag, ocean, basis, love):
    row_count = eta_tl.shape[0]
    lon_count = eta_tl.shape[1]
    lat_count = lax.axis_size("lat")
    total_rows = row_count * lat_count
    first_row = lax.axis_index("lat") * row_count
    indices = first_row + jnp.arange(row_count, dtype=jnp.int32)
    latitude = (indices.astype(jnp.float32) + 0.5) * (jnp.pi / total_rows) - 0.5 * jnp.pi
    cosine = jnp.cos(latitude)
    quad_weight = jnp.pi / total_rows * cosine
    east_factor = (kappa_x / (0.5 + 0.5 * cosine))[:, None]
    wet_mask = ocean.astype(jnp.float32)
    flux_north = kappa_y * wet_mask * eta_adj
    north_depth, north_wet, north_flux = edges_from(
        [depth[:1], wet_mask[:1], flux_north[:1]], -1
    )
    south_flux, south_depth, south_wet, south_drag, south_v, south_va = edges_from(
        [flux_north[-1:], depth[-1:], wet_mask[-1:], drag[-1:], vel_tl[1, -1:], vel_adj[1, -1:]], 1
    )
    south_mask = south_wet * wet_mask[:1]
    south_height = 0.5 * (south_depth + depth[:1])
    south_retain = 1.0 - south_drag
    depth_up = northward(depth, north_depth)
    wet_up = northward(wet_mask, north_wet)
    mask_u = wet_mask * jnp.roll(wet_mask, -1, 1)
    mask_v = wet_mask * wet_up
    depth_u = 0.5 * (depth + jnp.roll(depth, -1, 1))
    depth_v = 0.5 * (depth + depth_up)
    retain = 1.0 - drag
    ones_weight = jnp.ones_like(quad_weight)
    analysis_weight = jnp.stack([quad_weight, ones_weight])
    output_weight = jnp.stack([ones_weight, quad_weight])
    owned_count = basis.shape[0]
    order_total = owned_count * lat_count
    full_orders = jnp.arange(order_total, dtype=jnp.int32)
    tables = fourier_tables(lon_count, order_total)
    full_factor = order_factor(full_orders)
    state_eta, state_vel = (eta_tl, vel_tl)
    back_eta, back_vel = (eta_adj, vel_adj)

    def adjoint_terms(eta, vel, flux_edge, flux_below, va_below):
        flux_east = east_factor * wet_mask * eta
        flux_up = kappa_y * wet_mask * eta
        north_up = northward(flux_up, flux_edge)
        p_term = mask_u * (vel[0] + depth_u * (jnp.roll(flux_east, -1, 1) - flux_east))
        q_term = mask_v * (vel[1] + depth_v * (north_up - flux_up))
        q_below = south_mask * (va_below + south_height * (flux_up[:1] - flux_below))
        return p_term, q_term, q_below

    p_term, q_term, q_edge = adjoint_terms(back_eta, back_vel, north_flux, south_flux, south_va)
    for step_index in range(STEPS):
        flux_p = east_factor * p_term
        q_down = southward(q_term, q_edge)
        psi_bar = flux_p - jnp.roll(flux_p, 1, 1) + kappa_y * (q_term - q_down)
        spectra = analyse(jnp.stack([state_eta, psi_bar]), analysis_weight, tables, order_total)
        banded = load_spectra(spectra, basis, love, lat_count, lax.axis_size("deg"))
        loads = synthesise(banded, full_factor, tables, output_weight)
        last = step_index == STEPS - 1
        psi_now = state_eta - loads[0]
        back_eta = back_eta + psi_bar - loads[1]
        back_vel = (retain * p_term, retain * q_term)
        north_rows, south_rows = [psi_now[:1]], [psi_now[-1:]]
        if not last:
            flux_now = kappa_y * wet_mask * back_eta
            north_rows.append(flux_now[:1])
            south_rows.append(flux_now[-1:])
        north_edges = edges_from(north_rows, -1)
        south_edges = edges_from(south_rows, 1)
        psi_up = northward(psi_now, north_edges[0])
        new_u = mask_u * (
            retain * state_vel[0] - east_factor * (jnp.roll(psi_now, -1, 1) - psi_now)
        )
        new_v = mask_v * (retain * state_vel[1] - kappa_y * (psi_up - psi_now))
        flux_x = depth_u * new_u
        flux_y = depth_v * new_v
        south_v = south_mask * (south_retain * south_v - kappa_y * (psi_now[:1] - south_edges[0]))
        flux_down = southward(flux_y, south_height * south_v)
        if not last:
            south_va = south_retain * q_edge
            p_term, q_term, q_edge = adjoint_terms(
                back_eta, back_vel, north_edges[1], south_edges[1], south_va
            )
        state_eta = state_eta - wet_mask * (
            east_factor * (flux_x - jnp.roll(flux_x, 1, 1)) + kappa_y * (flux_y - flux_down)
        )
        state_vel = (new_u, new_v)
    state_vel, back_vel = jnp.stack(state_vel), jnp.stack(back_vel)
    return (state_eta, state_vel, back_eta, back_vel)


def solution(mesh):
    in_specs = (
        P("lat", None),
        P(None, "lat", None),
        P("lat", None),
        P(None, "lat", None),
        P("lat", None),
        P("lat", None),
        P("lat", None),
        P("lat", None, "deg"),
        P("deg"),
    )
    out_specs = (P("lat", None), P(None, "lat", None), P("lat", None), P(None, "lat", None))
    return jax.shard_map(
        on_device, mesh=mesh, in_specs=in_specs, out_specs=out_specs, check_vma=False
    )
```

```python
import functools
import jax
import jax.numpy as jnp
import numpy as np
from jax import lax
from jax.experimental import pallas as pl
from jax.experimental.pallas import tpu as pltpu
from jax.sharding import PartitionSpec as P

STEPS = 2
LANES = 128
GROUP = 32


kappa_x = 0.3
kappa_y = 0.4


def passed_along(value, axis, by):
    length = lax.axis_size(axis)
    pairs = [(i, i + by) for i in range(length) if 0 <= i + by < length]
    return lax.ppermute(value, axis, pairs)


def circle(numerator, period):
    angles = 2.0 * np.pi * (numerator % period) / period
    return np.cos(angles), np.sin(angles)


def fourier_tables(lon_count, order_total):
    major = lon_count // LANES
    blocks = -(-order_total // major)
    residues, lanes = np.arange(major), np.arange(LANES)
    outer = np.stack(circle(residues[:, None] * residues[None, :], major))
    turn = np.stack(circle(residues[:, None] * lanes[None, :], lon_count))
    inner = np.stack(circle(np.arange(blocks)[:, None] * lanes[None, :], LANES))
    return (
        jnp.asarray(outer, jnp.bfloat16),
        jnp.asarray(turn, jnp.float32),
        jnp.asarray(inner, jnp.bfloat16),
    )


def order_factor(orders):
    return jnp.where(orders == 0, 1.0, 2.0).astype(jnp.bfloat16)


def analyse(stacked, analysis_weight, tables, order_count):
    outer, turn, inner = tables
    row_count = stacked.shape[1]
    lon_count = stacked.shape[2]
    split_rows = stacked.astype(jnp.bfloat16).reshape(2 * row_count, lon_count // LANES, LANES)
    first = jnp.einsum("cka,rab->crkb", outer, split_rows, preferred_element_type=jnp.float32)
    turned = jnp.stack(
        [first[0] * turn[0] - first[1] * turn[1], first[1] * turn[0] + first[0] * turn[1]]
    ).astype(jnp.bfloat16)
    second = jnp.stack([jnp.stack([inner[0], -inner[1]]), jnp.stack([inner[1], inner[0]])])
    spectra = jnp.einsum("crkb,dcnb->drnk", turned, second, preferred_element_type=jnp.float32)
    spectra = spectra.reshape(2, 2, row_count, -1)[..., :order_count] * (1.0 / lon_count)
    return (spectra * analysis_weight[None, :, :, None]).astype(jnp.bfloat16)


def synthesise(coeffs, factors, tables, output_weight):
    outer, turn, inner = tables
    major, blocks = turn.shape[1], inner.shape[1]
    row_count, order_count = coeffs.shape[2:]
    scaled = (coeffs * factors).reshape(2, 2 * row_count, order_count)
    padded = jnp.pad(scaled, ((0, 0), (0, 0), (0, major * blocks - order_count)))
    padded = padded.reshape(2, 2 * row_count, blocks, major)
    second = jnp.stack([jnp.stack([inner[0], inner[1]]), jnp.stack([-inner[1], inner[0]])])
    first = jnp.einsum("crnk,dcnb->drkb", padded, second, preferred_element_type=jnp.float32)
    turned = jnp.stack(
        [first[0] * turn[0] + first[1] * turn[1], first[1] * turn[0] - first[0] * turn[1]]
    ).astype(jnp.bfloat16)
    grid_out = jnp.einsum("cka,crkb->rab", outer, turned, preferred_element_type=jnp.float32)
    return grid_out.reshape(2, row_count, -1) * output_weight[:, :, None]


def greet(count, device_of):
    barrier = pltpu.get_barrier_semaphore()

    def one(step, carry):
        pl.semaphore_signal(
            barrier, inc=1, device_id=device_of(step), device_id_type=pl.DeviceIdType.MESH
        )
        return carry

    lax.fori_loop(1, count, one, 0)
    pl.semaphore_wait(barrier, count - 1)


def swap(count, copy_of):
    def begin(step, carry):
        copy_of(step).start()
        return carry

    def finish(step, carry):
        copy_of(step).wait()
        return carry

    lax.fori_loop(1, count, begin, 0)
    return lambda: lax.fori_loop(1, count, finish, 0)


def load_kernel(
    sizes, send_ref, basis_ref, love_ref, out_ref, basis, landed, ready, held,
    basis_sem, spread_out, spread_in, gather_out, gather_in,
):
    lat_count, deg_count, row_count, halves, cluster = sizes
    tall = 4 * cluster
    count = lat_count * deg_count
    total_rows = lat_count * row_count
    me_lat, me_deg = lax.axis_index("lat"), lax.axis_index("deg")
    me = me_lat * deg_count + me_deg

    def band_of(step):
        return (lax.rem(me_lat + step, lat_count), me_deg)

    def device_of(step):
        peer = lax.rem(me + step, count)
        return (lax.div(peer, deg_count), lax.rem(peer, deg_count))

    def spread_copy(step):
        peer = band_of(step)
        return pltpu.make_async_remote_copy(
            src_ref=send_ref.at[peer[0]],
            dst_ref=landed.at[me_lat],
            send_sem=spread_out.at[step - 1],
            recv_sem=spread_in.at[step - 1],
            device_id=peer,
            device_id_type=pl.DeviceIdType.MESH,
        )

    def gather_copy(step):
        peer = device_of(step)
        return pltpu.make_async_remote_copy(
            src_ref=ready.at[peer[0]],
            dst_ref=held.at[me],
            send_sem=gather_out.at[step - 1],
            recv_sem=gather_in.at[step - 1],
            device_id=peer,
            device_id_type=pl.DeviceIdType.MESH,
        )

    fetch = pltpu.make_async_copy(basis_ref, basis, basis_sem)
    fetch.start()
    greet(count, device_of)
    finish = swap(lat_count, spread_copy)
    landed[me_lat] = send_ref[me_lat]
    finish()
    fetch.wait()

    copies = max(1, LANES // total_rows)
    width = copies * total_rows
    row_order = lax.broadcasted_iota(jnp.int32, (tall, width), 0) % cluster
    lane_part = lax.broadcasted_iota(jnp.int32, (tall, width), 1) // total_rows
    chunk = min(cluster, max(copies, 2048 // total_rows))
    blocks = [landed[source].astype(jnp.float32) for source in range(lat_count)]
    groups = blocks[0].shape[1] // tall
    love = love_ref[...]
    done = []
    for half in range(halves):
        for group in range(groups):
            first = (half * groups + group) * cluster
            lanes = slice(group * tall, (group + 1) * tall)
            rows = slice(half * row_count, (half + 1) * row_count)
            tile = jnp.concatenate([block[rows, lanes] for block in blocks], 0).T
            tile = jnp.concatenate([tile] * copies, 1)
            masks = [row_order == order + lane_part for order in range(0, cluster, copies)]
            total = jnp.zeros((tall, love.shape[1]), jnp.float32)
            for start in range(0, cluster, chunk):
                spaced = jnp.concatenate(
                    [
                        jnp.where(masks[order // copies], tile, 0.0).astype(jnp.bfloat16)
                        for order in range(start, start + chunk, copies)
                    ],
                    1,
                )
                part = basis[first + start : first + start + chunk]
                part = part.reshape(chunk * total_rows, love.shape[1])
                total = total + jnp.dot(spaced, part, preferred_element_type=jnp.float32)
            scaled = (total * love).astype(jnp.bfloat16)
            merged = jnp.zeros((tall, width), jnp.float32)
            for start in range(0, cluster, chunk):
                part = basis[first + start : first + start + chunk]
                part = part.reshape(chunk * total_rows, love.shape[1])
                wide = lax.dot_general(
                    scaled, part, (((1,), (1,)), ((), ())), preferred_element_type=jnp.float32
                )
                for step in range(chunk // copies):
                    mask = masks[start // copies + step]
                    merged = merged + jnp.where(
                        mask, wide[:, step * width : (step + 1) * width], 0.0
                    )
            summed = merged[:, :total_rows]
            for copy in range(1, copies):
                summed = summed + merged[:, copy * total_rows : (copy + 1) * total_rows]
            done.append(summed.T)
    for band in range(lat_count):
        rows = slice(band * row_count, (band + 1) * row_count)
        lines = [
            jnp.concatenate([done[half * groups + g][rows] for g in range(groups)], 1)
            for half in range(halves)
        ]
        ready[band] = jnp.concatenate(lines, 0).astype(jnp.bfloat16)
    finish = swap(count, gather_copy)
    held[me] = ready[me_lat]
    finish()
    for source in range(lat_count):
        total = held[source * deg_count].astype(jnp.float32)
        for part in range(1, deg_count):
            total = total + held[source * deg_count + part].astype(jnp.float32)
        out_ref[source] = total.astype(out_ref.dtype)


def load_spectra(spectra, basis, love, lat_count, deg_count):
    row_count, order_total = spectra.shape[2:]
    owned = order_total // lat_count
    halves = max(1, 16 // row_count)
    cluster = min(GROUP, owned // halves)
    groups = owned // (halves * cluster)
    split = spectra.reshape(2, 2, row_count, lat_count, halves, groups, cluster)
    blocks = split.transpose(3, 4, 2, 5, 0, 1, 6)
    blocks = blocks.reshape(lat_count, halves * row_count, groups * 4 * cluster)
    count = lat_count * deg_count
    vmem = pl.BlockSpec(memory_space=pltpu.VMEM)
    got = pl.pallas_call(
        functools.partial(load_kernel, (lat_count, deg_count, row_count, halves, cluster)),
        out_shape=jax.ShapeDtypeStruct(blocks.shape, blocks.dtype),
        in_specs=[vmem, pl.BlockSpec(memory_space=pl.ANY), vmem],
        out_specs=vmem,
        scratch_shapes=[
            pltpu.VMEM(basis.shape, basis.dtype),
            pltpu.VMEM(blocks.shape, blocks.dtype),
            pltpu.VMEM(blocks.shape, blocks.dtype),
            pltpu.VMEM((count,) + blocks.shape[1:], blocks.dtype),
            pltpu.SemaphoreType.DMA,
            pltpu.SemaphoreType.DMA((lat_count - 1,)),
            pltpu.SemaphoreType.DMA((lat_count - 1,)),
            pltpu.SemaphoreType.DMA((count - 1,)),
            pltpu.SemaphoreType.DMA((count - 1,)),
        ],
        compiler_params=pltpu.CompilerParams(
            collective_id=0, has_side_effects=True, vmem_limit_bytes=56 * 2**20
        ),
    )(blocks, basis, love[None, :])
    got = got.reshape(lat_count, halves, row_count, groups, 2, 2, cluster)
    return got.transpose(4, 5, 2, 0, 1, 3, 6).reshape(spectra.shape)


def edges_from(rows, by):
    sent = jnp.concatenate(rows, 0).astype(jnp.bfloat16)
    got = passed_along(sent, "lat", by).astype(jnp.float32)
    return [got[i : i + 1] for i in range(len(rows))]


def northward(values, edge):
    return jnp.concatenate([values[1:], edge], 0)


def southward(values, edge):
    return jnp.concatenate([edge, values[:-1]], 0)


def on_device(eta_tl, vel_tl, eta_adj, vel_adj, depth, drag, ocean, basis, love):
    row_count = eta_tl.shape[0]
    lon_count = eta_tl.shape[1]
    lat_count = lax.axis_size("lat")
    total_rows = row_count * lat_count
    first_row = lax.axis_index("lat") * row_count
    indices = first_row + jnp.arange(row_count, dtype=jnp.int32)
    latitude = (indices.astype(jnp.float32) + 0.5) * (jnp.pi / total_rows) - 0.5 * jnp.pi
    cosine = jnp.cos(latitude)
    quad_weight = jnp.pi / total_rows * cosine
    east_factor = (kappa_x / (0.5 + 0.5 * cosine))[:, None]
    wet_mask = ocean.astype(jnp.float32)
    flux_north = kappa_y * wet_mask * eta_adj
    north_depth, north_wet, north_flux = edges_from(
        [depth[:1], wet_mask[:1], flux_north[:1]], -1
    )
    south_flux, south_depth, south_wet, south_drag, south_v, south_va = edges_from(
        [flux_north[-1:], depth[-1:], wet_mask[-1:], drag[-1:], vel_tl[1, -1:], vel_adj[1, -1:]], 1
    )
    south_mask = south_wet * wet_mask[:1]
    south_height = 0.5 * (south_depth + depth[:1])
    south_retain = 1.0 - south_drag
    depth_up = northward(depth, north_depth)
    wet_up = northward(wet_mask, north_wet)
    mask_u = wet_mask * jnp.roll(wet_mask, -1, 1)
    mask_v = wet_mask * wet_up
    depth_u = 0.5 * (depth + jnp.roll(depth, -1, 1))
    depth_v = 0.5 * (depth + depth_up)
    retain = 1.0 - drag
    ones_weight = jnp.ones_like(quad_weight)
    analysis_weight = jnp.stack([quad_weight, ones_weight])
    output_weight = jnp.stack([ones_weight, quad_weight])
    owned_count = basis.shape[0]
    order_total = owned_count * lat_count
    full_orders = jnp.arange(order_total, dtype=jnp.int32)
    tables = fourier_tables(lon_count, order_total)
    full_factor = order_factor(full_orders)
    state_eta, state_vel = (eta_tl, vel_tl)
    back_eta, back_vel = (eta_adj, vel_adj)

    def adjoint_terms(eta, vel, flux_edge, flux_below, va_below):
        flux_east = east_factor * wet_mask * eta
        flux_up = kappa_y * wet_mask * eta
        north_up = northward(flux_up, flux_edge)
        p_term = mask_u * (vel[0] + depth_u * (jnp.roll(flux_east, -1, 1) - flux_east))
        q_term = mask_v * (vel[1] + depth_v * (north_up - flux_up))
        q_below = south_mask * (va_below + south_height * (flux_up[:1] - flux_below))
        return p_term, q_term, q_below

    p_term, q_term, q_edge = adjoint_terms(back_eta, back_vel, north_flux, south_flux, south_va)
    for step_index in range(STEPS):
        flux_p = east_factor * p_term
        q_down = southward(q_term, q_edge)
        psi_bar = flux_p - jnp.roll(flux_p, 1, 1) + kappa_y * (q_term - q_down)
        spectra = analyse(jnp.stack([state_eta, psi_bar]), analysis_weight, tables, order_total)
        banded = load_spectra(spectra, basis, love, lat_count, lax.axis_size("deg"))
        loads = synthesise(banded, full_factor, tables, output_weight)
        last = step_index == STEPS - 1
        psi_now = state_eta - loads[0]
        back_eta = back_eta + psi_bar - loads[1]
        back_vel = (retain * p_term, retain * q_term)
        north_rows, south_rows = [psi_now[:1]], [psi_now[-1:]]
        if not last:
            flux_now = kappa_y * wet_mask * back_eta
            north_rows.append(flux_now[:1])
            south_rows.append(flux_now[-1:])
        north_edges = edges_from(north_rows, -1)
        south_edges = edges_from(south_rows, 1)
        psi_up = northward(psi_now, north_edges[0])
        new_u = mask_u * (
            retain * state_vel[0] - east_factor * (jnp.roll(psi_now, -1, 1) - psi_now)
        )
        new_v = mask_v * (retain * state_vel[1] - kappa_y * (psi_up - psi_now))
        flux_x = depth_u * new_u
        flux_y = depth_v * new_v
        south_v = south_mask * (south_retain * south_v - kappa_y * (psi_now[:1] - south_edges[0]))
        flux_down = southward(flux_y, south_height * south_v)
        if not last:
            south_va = south_retain * q_edge
            p_term, q_term, q_edge = adjoint_terms(
                back_eta, back_vel, north_edges[1], south_edges[1], south_va
            )
        state_eta = state_eta - wet_mask * (
            east_factor * (flux_x - jnp.roll(flux_x, 1, 1)) + kappa_y * (flux_y - flux_down)
        )
        state_vel = (new_u, new_v)
    state_vel, back_vel = jnp.stack(state_vel), jnp.stack(back_vel)
    return (state_eta, state_vel, back_eta, back_vel)


def solution(mesh):
    in_specs = (
        P("lat", None),
        P(None, "lat", None),
        P("lat", None),
        P(None, "lat", None),
        P("lat", None),
        P("lat", None),
        P("lat", None),
        P("lat", None, "deg"),
        P("deg"),
    )
    out_specs = (P("lat", None), P(None, "lat", None), P("lat", None), P(None, "lat", None))
    return jax.shard_map(
        on_device, mesh=mesh, in_specs=in_specs, out_specs=out_specs, check_vma=False
    )
```

```python
import functools
import jax
import jax.numpy as jnp
import numpy as np
from jax import lax
from jax.experimental import pallas as pl
from jax.experimental.pallas import tpu as pltpu
from jax.sharding import PartitionSpec as P

STEPS = 2
LANES = 128
GROUP = 32


kappa_x = 0.3
kappa_y = 0.4


def passed_along(value, axis, by):
    length = lax.axis_size(axis)
    pairs = [(i, i + by) for i in range(length) if 0 <= i + by < length]
    return lax.ppermute(value, axis, pairs)


def circle(numerator, period):
    angles = 2.0 * np.pi * (numerator % period) / period
    return np.cos(angles), np.sin(angles)


def fourier_tables(lon_count, order_total):
    major = lon_count // LANES
    blocks = -(-order_total // major)
    residues, lanes = np.arange(major), np.arange(LANES)
    outer = np.stack(circle(residues[:, None] * residues[None, :], major))
    turn = np.stack(circle(residues[:, None] * lanes[None, :], lon_count))
    inner = np.stack(circle(np.arange(blocks)[:, None] * lanes[None, :], LANES))
    return (
        jnp.asarray(outer, jnp.bfloat16),
        jnp.asarray(turn, jnp.float32),
        jnp.asarray(inner, jnp.bfloat16),
    )


def order_factor(orders):
    return jnp.where(orders == 0, 1.0, 2.0).astype(jnp.bfloat16)


def analyse(stacked, analysis_weight, tables, order_count):
    outer, turn, inner = tables
    row_count = stacked.shape[1]
    lon_count = stacked.shape[2]
    split_rows = stacked.astype(jnp.bfloat16).reshape(2 * row_count, lon_count // LANES, LANES)
    first = jnp.einsum("cka,rab->crkb", outer, split_rows, preferred_element_type=jnp.float32)
    turned = jnp.stack(
        [first[0] * turn[0] - first[1] * turn[1], first[1] * turn[0] + first[0] * turn[1]]
    ).astype(jnp.bfloat16)
    second = jnp.stack([jnp.stack([inner[0], -inner[1]]), jnp.stack([inner[1], inner[0]])])
    spectra = jnp.einsum("crkb,dcnb->drnk", turned, second, preferred_element_type=jnp.float32)
    spectra = spectra.reshape(2, 2, row_count, -1)[..., :order_count] * (1.0 / lon_count)
    return (spectra * analysis_weight[None, :, :, None]).astype(jnp.bfloat16)


def synthesise(coeffs, factors, tables, output_weight):
    outer, turn, inner = tables
    major, blocks = turn.shape[1], inner.shape[1]
    row_count, order_count = coeffs.shape[2:]
    scaled = (coeffs * factors).reshape(2, 2 * row_count, order_count)
    padded = jnp.pad(scaled, ((0, 0), (0, 0), (0, major * blocks - order_count)))
    padded = padded.reshape(2, 2 * row_count, blocks, major)
    second = jnp.stack([jnp.stack([inner[0], inner[1]]), jnp.stack([-inner[1], inner[0]])])
    first = jnp.einsum("crnk,dcnb->drkb", padded, second, preferred_element_type=jnp.float32)
    turned = jnp.stack(
        [first[0] * turn[0] + first[1] * turn[1], first[1] * turn[0] - first[0] * turn[1]]
    ).astype(jnp.bfloat16)
    grid_out = jnp.einsum("cka,crkb->rab", outer, turned, preferred_element_type=jnp.float32)
    return grid_out.reshape(2, row_count, -1) * output_weight[:, :, None]


def greet(count, device_of):
    barrier = pltpu.get_barrier_semaphore()

    def one(step, carry):
        pl.semaphore_signal(
            barrier, inc=1, device_id=device_of(step), device_id_type=pl.DeviceIdType.MESH
        )
        return carry

    lax.fori_loop(1, count, one, 0, unroll=count <= 32)
    pl.semaphore_wait(barrier, count - 1)


def swap(count, copy_of):
    def begin(step, carry):
        copy_of(step).start()
        return carry

    def finish(step, carry):
        copy_of(step).wait()
        return carry

    lax.fori_loop(1, count, begin, 0, unroll=count <= 32)
    return lambda: lax.fori_loop(1, count, finish, 0)


def load_kernel(
    sizes, send_ref, basis_ref, love_ref, out_ref, basis, landed, ready, held,
    basis_sem, spread_out, spread_in, gather_out, gather_in,
):
    lat_count, deg_count, row_count, halves, cluster = sizes
    tall = 4 * cluster
    count = lat_count * deg_count
    total_rows = lat_count * row_count
    me_lat, me_deg = lax.axis_index("lat"), lax.axis_index("deg")
    me = me_lat * deg_count + me_deg

    def band_of(step):
        return (lax.rem(me_lat + step, lat_count), me_deg)

    def device_of(step):
        peer = lax.rem(me + step, count)
        return (lax.div(peer, deg_count), lax.rem(peer, deg_count))

    def spread_copy(step):
        peer = band_of(step)
        return pltpu.make_async_remote_copy(
            src_ref=send_ref.at[peer[0]],
            dst_ref=landed.at[me_lat],
            send_sem=spread_out.at[step - 1],
            recv_sem=spread_in.at[step - 1],
            device_id=peer,
            device_id_type=pl.DeviceIdType.MESH,
        )

    def gather_copy(step):
        peer = device_of(step)
        return pltpu.make_async_remote_copy(
            src_ref=ready.at[peer[0]],
            dst_ref=held.at[me],
            send_sem=gather_out.at[step - 1],
            recv_sem=gather_in.at[step - 1],
            device_id=peer,
            device_id_type=pl.DeviceIdType.MESH,
        )

    fetch = pltpu.make_async_copy(basis_ref, basis, basis_sem)
    fetch.start()
    greet(count, device_of)
    finish = swap(lat_count, spread_copy)
    landed[me_lat] = send_ref[me_lat]
    finish()
    fetch.wait()

    copies = max(1, LANES // total_rows)
    width = copies * total_rows
    row_order = lax.broadcasted_iota(jnp.int32, (tall, width), 0) % cluster
    lane_part = lax.broadcasted_iota(jnp.int32, (tall, width), 1) // total_rows
    chunk = min(cluster, max(copies, 2048 // total_rows))
    blocks = [landed[source].astype(jnp.float32) for source in range(lat_count)]
    groups = blocks[0].shape[1] // tall
    love = love_ref[...]
    done = []
    for half in range(halves):
        for group in range(groups):
            first = (half * groups + group) * cluster
            lanes = slice(group * tall, (group + 1) * tall)
            rows = slice(half * row_count, (half + 1) * row_count)
            tile = jnp.concatenate([block[rows, lanes] for block in blocks], 0).T
            tile = jnp.concatenate([tile] * copies, 1)
            masks = [row_order == order + lane_part for order in range(0, cluster, copies)]
            total = jnp.zeros((tall, love.shape[1]), jnp.float32)
            for start in range(0, cluster, chunk):
                spaced = jnp.concatenate(
                    [
                        jnp.where(masks[order // copies], tile, 0.0).astype(jnp.bfloat16)
                        for order in range(start, start + chunk, copies)
                    ],
                    1,
                )
                part = basis[first + start : first + start + chunk]
                part = part.reshape(chunk * total_rows, love.shape[1])
                total = total + jnp.dot(spaced, part, preferred_element_type=jnp.float32)
            scaled = (total * love).astype(jnp.bfloat16)
            merged = jnp.zeros((tall, width), jnp.float32)
            for start in range(0, cluster, chunk):
                part = basis[first + start : first + start + chunk]
                part = part.reshape(chunk * total_rows, love.shape[1])
                wide = lax.dot_general(
                    scaled, part, (((1,), (1,)), ((), ())), preferred_element_type=jnp.float32
                )
                for step in range(chunk // copies):
                    mask = masks[start // copies + step]
                    merged = merged + jnp.where(
                        mask, wide[:, step * width : (step + 1) * width], 0.0
                    )
            summed = merged[:, :total_rows]
            for copy in range(1, copies):
                summed = summed + merged[:, copy * total_rows : (copy + 1) * total_rows]
            done.append(summed.T)
    for band in range(lat_count):
        rows = slice(band * row_count, (band + 1) * row_count)
        lines = [
            jnp.concatenate([done[half * groups + g][rows] for g in range(groups)], 1)
            for half in range(halves)
        ]
        ready[band] = jnp.concatenate(lines, 0).astype(jnp.bfloat16)
    finish = swap(count, gather_copy)
    held[me] = ready[me_lat]
    finish()
    for source in range(lat_count):
        total = held[source * deg_count].astype(jnp.float32)
        for part in range(1, deg_count):
            total = total + held[source * deg_count + part].astype(jnp.float32)
        out_ref[source] = total.astype(out_ref.dtype)


def load_spectra(spectra, basis, love, lat_count, deg_count):
    row_count, order_total = spectra.shape[2:]
    owned = order_total // lat_count
    halves = max(1, 16 // row_count)
    cluster = min(GROUP, owned // halves)
    groups = owned // (halves * cluster)
    split = spectra.reshape(2, 2, row_count, lat_count, halves, groups, cluster)
    blocks = split.transpose(3, 4, 2, 5, 0, 1, 6)
    blocks = blocks.reshape(lat_count, halves * row_count, groups * 4 * cluster)
    count = lat_count * deg_count
    vmem = pl.BlockSpec(memory_space=pltpu.VMEM)
    got = pl.pallas_call(
        functools.partial(load_kernel, (lat_count, deg_count, row_count, halves, cluster)),
        out_shape=jax.ShapeDtypeStruct(blocks.shape, blocks.dtype),
        in_specs=[vmem, pl.BlockSpec(memory_space=pl.ANY), vmem],
        out_specs=vmem,
        scratch_shapes=[
            pltpu.VMEM(basis.shape, basis.dtype),
            pltpu.VMEM(blocks.shape, blocks.dtype),
            pltpu.VMEM(blocks.shape, blocks.dtype),
            pltpu.VMEM((count,) + blocks.shape[1:], blocks.dtype),
            pltpu.SemaphoreType.DMA,
            pltpu.SemaphoreType.DMA((lat_count - 1,)),
            pltpu.SemaphoreType.DMA((lat_count - 1,)),
            pltpu.SemaphoreType.DMA((count - 1,)),
            pltpu.SemaphoreType.DMA((count - 1,)),
        ],
        compiler_params=pltpu.CompilerParams(
            collective_id=0, has_side_effects=True, vmem_limit_bytes=40 * 2**20
        ),
    )(blocks, basis, love[None, :])
    got = got.reshape(lat_count, halves, row_count, groups, 2, 2, cluster)
    return got.transpose(4, 5, 2, 0, 1, 3, 6).reshape(spectra.shape)


def edges_from(rows, by):
    sent = jnp.concatenate(rows, 0).astype(jnp.bfloat16)
    got = passed_along(sent, "lat", by).astype(jnp.float32)
    return [got[i : i + 1] for i in range(len(rows))]


def northward(values, edge):
    return jnp.concatenate([values[1:], edge], 0)


def southward(values, edge):
    return jnp.concatenate([edge, values[:-1]], 0)


def on_device(eta_tl, vel_tl, eta_adj, vel_adj, depth, drag, ocean, basis, love):
    row_count = eta_tl.shape[0]
    lon_count = eta_tl.shape[1]
    lat_count = lax.axis_size("lat")
    total_rows = row_count * lat_count
    first_row = lax.axis_index("lat") * row_count
    indices = first_row + jnp.arange(row_count, dtype=jnp.int32)
    latitude = (indices.astype(jnp.float32) + 0.5) * (jnp.pi / total_rows) - 0.5 * jnp.pi
    cosine = jnp.cos(latitude)
    quad_weight = jnp.pi / total_rows * cosine
    east_factor = (kappa_x / (0.5 + 0.5 * cosine))[:, None]
    wet_mask = ocean.astype(jnp.float32)
    flux_north = kappa_y * wet_mask * eta_adj
    north_depth, north_wet, north_flux = edges_from(
        [depth[:1], wet_mask[:1], flux_north[:1]], -1
    )
    south_flux, south_depth, south_wet, south_drag, south_v, south_va = edges_from(
        [flux_north[-1:], depth[-1:], wet_mask[-1:], drag[-1:], vel_tl[1, -1:], vel_adj[1, -1:]], 1
    )
    south_mask = south_wet * wet_mask[:1]
    south_height = 0.5 * (south_depth + depth[:1])
    south_retain = 1.0 - south_drag
    depth_up = northward(depth, north_depth)
    wet_up = northward(wet_mask, north_wet)
    mask_u = wet_mask * jnp.roll(wet_mask, -1, 1)
    mask_v = wet_mask * wet_up
    depth_u = 0.5 * (depth + jnp.roll(depth, -1, 1))
    depth_v = 0.5 * (depth + depth_up)
    retain = 1.0 - drag
    ones_weight = jnp.ones_like(quad_weight)
    analysis_weight = jnp.stack([quad_weight, ones_weight])
    output_weight = jnp.stack([ones_weight, quad_weight])
    owned_count = basis.shape[0]
    order_total = owned_count * lat_count
    full_orders = jnp.arange(order_total, dtype=jnp.int32)
    tables = fourier_tables(lon_count, order_total)
    full_factor = order_factor(full_orders)
    state_eta, state_vel = (eta_tl, vel_tl)
    back_eta, back_vel = (eta_adj, vel_adj)

    def adjoint_terms(eta, vel, flux_edge, flux_below, va_below):
        flux_east = east_factor * wet_mask * eta
        flux_up = kappa_y * wet_mask * eta
        north_up = northward(flux_up, flux_edge)
        p_term = mask_u * (vel[0] + depth_u * (jnp.roll(flux_east, -1, 1) - flux_east))
        q_term = mask_v * (vel[1] + depth_v * (north_up - flux_up))
        q_below = south_mask * (va_below + south_height * (flux_up[:1] - flux_below))
        return p_term, q_term, q_below

    p_term, q_term, q_edge = adjoint_terms(back_eta, back_vel, north_flux, south_flux, south_va)
    for step_index in range(STEPS):
        flux_p = east_factor * p_term
        q_down = southward(q_term, q_edge)
        psi_bar = flux_p - jnp.roll(flux_p, 1, 1) + kappa_y * (q_term - q_down)
        spectra = analyse(jnp.stack([state_eta, psi_bar]), analysis_weight, tables, order_total)
        banded = load_spectra(spectra, basis, love, lat_count, lax.axis_size("deg"))
        loads = synthesise(banded, full_factor, tables, output_weight)
        last = step_index == STEPS - 1
        psi_now = state_eta - loads[0]
        back_eta = back_eta + psi_bar - loads[1]
        back_vel = (retain * p_term, retain * q_term)
        north_rows, south_rows = [psi_now[:1]], [psi_now[-1:]]
        if not last:
            flux_now = kappa_y * wet_mask * back_eta
            north_rows.append(flux_now[:1])
            south_rows.append(flux_now[-1:])
        north_edges = edges_from(north_rows, -1)
        south_edges = edges_from(south_rows, 1)
        psi_up = northward(psi_now, north_edges[0])
        new_u = mask_u * (
            retain * state_vel[0] - east_factor * (jnp.roll(psi_now, -1, 1) - psi_now)
        )
        new_v = mask_v * (retain * state_vel[1] - kappa_y * (psi_up - psi_now))
        flux_x = depth_u * new_u
        flux_y = depth_v * new_v
        south_v = south_mask * (south_retain * south_v - kappa_y * (psi_now[:1] - south_edges[0]))
        flux_down = southward(flux_y, south_height * south_v)
        if not last:
            south_va = south_retain * q_edge
            p_term, q_term, q_edge = adjoint_terms(
                back_eta, back_vel, north_edges[1], south_edges[1], south_va
            )
        state_eta = state_eta - wet_mask * (
            east_factor * (flux_x - jnp.roll(flux_x, 1, 1)) + kappa_y * (flux_y - flux_down)
        )
        state_vel = (new_u, new_v)
    state_vel, back_vel = jnp.stack(state_vel), jnp.stack(back_vel)
    return (state_eta, state_vel, back_eta, back_vel)


def solution(mesh):
    in_specs = (
        P("lat", None),
        P(None, "lat", None),
        P("lat", None),
        P(None, "lat", None),
        P("lat", None),
        P("lat", None),
        P("lat", None),
        P("lat", None, "deg"),
        P("deg"),
    )
    out_specs = (P("lat", None), P(None, "lat", None), P("lat", None), P(None, "lat", None))
    return jax.shard_map(
        on_device, mesh=mesh, in_specs=in_specs, out_specs=out_specs, check_vma=False
    )
```
